256 devices in a mesh: slide: 8 (over x, y_hi), tile: 32 (over y_lo, z, core).
Axes of the slice: x: 4, y: 4 (y_hi: 2, y_lo: 2; y = y_hi * 2 + y_lo), z: 8, core: 2. Of those that a mesh axis runs over, the one named last changes fastest.
Arguments:
- slide_tiles: bfloat16 [8, 1024, 16, 16, 256], P('slide', 'tile'), may hold values from -6 to 6
- balance_list: int32 [8, 1024], P('slide'), may hold values from -1 to 575, as said below
- output_grad: bfloat16 [8, 1024, 8, 8, 512], P('slide', 'tile'), may hold values from -6 to 6
- w_reduce: bfloat16 [256, 128], replicated, may hold values from -0.375 to 0.375
- w_spatial: bfloat16 [1152, 128], replicated, may hold values from -0.1875 to 0.1875
- w_expand: bfloat16 [128, 512], replicated, may hold values from -0.5 to 0.5
- w_shortcut: bfloat16 [256, 512], replicated, may hold values from -0.375 to 0.375
Outputs:
- input_grad: bfloat16 [8, 1024, 16, 16, 256], P('slide', 'tile')
- grad_reduce: float32 [256, 128], replicated
- grad_spatial: float32 [1152, 128], replicated
- grad_expand: float32 [128, 512], replicated
- grad_shortcut: float32 [256, 512], replicated
The draws below stay inside these ranges and needn't reach their ends.
Inputs may be any that keep to these rules, and one draw needn't show every extreme that they name: `balance_list`: block b of a slide belongs to grid row b // 32. Entry w * 18 + s says that device w of the tile axis computes the block as its s-th; every value from 0 to 575 appears exactly once in each slide, the rest are -1. The blocks of one grid row that go to one device are at most 1, and some row sends exactly 1 to a device in every slide.
All inputs are finite; a program needn't handle non-finite values.
Results may differ from the reference program's by a relative error of at most 0.0066.
Values may be sent and summed in bfloat16 or wider, within the bound.
A program may use at most 128 MiB of HBM per device.

```python
import jax
import jax.numpy as jnp
from jax import lax

C_IN = 256
C_MID = 128
C_OUT = 512
P_SIZE = 16
OWN = 32
WORK = 18
HALF = 8
BLOCKS = 1024
SLIDES = 8
N_TILE = 32


def balance_one(slide_key):
    key_rows, key_order, key_cols, key_workers = jax.random.split(slide_key, 4)
    half_rows = N_TILE // 2
    spread = jax.random.randint(key_rows, (half_rows,), 0, OWN - WORK + 1)
    spread = spread.at[0].set(OWN - WORK)
    counts = jnp.concatenate([WORK + spread, WORK - spread])
    counts = counts[jax.random.permutation(key_order, N_TILE)]
    col_keys = jax.random.split(key_cols, N_TILE)
    ranks = jax.vmap(lambda row_key: jax.random.permutation(row_key, OWN))(col_keys)
    tissue = (ranks < counts[:, None]).reshape(-1).astype(jnp.int32)
    order = jnp.cumsum(tissue) - 1
    workers = jax.random.permutation(key_workers, N_TILE)
    target = workers[order % N_TILE] * WORK + order // N_TILE
    return jnp.where(tissue > 0, target, -1).astype(jnp.int32)


def draw_balance_list(key, part):
    slide_keys = jax.random.split(jax.random.fold_in(key, 11), SLIDES)
    return jax.vmap(balance_one)(slide_keys)


def levels(stream_key, shape, cuts, least, top_value):
    level = 1.0
    for dim, blocks in cuts:
        heights = jax.random.uniform(jax.random.fold_in(jax.random.fold_in(stream_key, 6), dim), (blocks,), jnp.float32, least / len(cuts), top_value / len(cuts))
        level = level * jnp.repeat(jnp.exp(heights), shape[dim] // blocks).reshape((-1,) + (1,) * (len(shape) - 1 - dim))
    return level


def scatter_about(key, shape, scale, most, cuts=(), held_as=jnp.bfloat16):
    entries = scale * jax.random.normal(key, shape, jnp.float32)
    if cuts:
        entries = entries * levels(key, shape, cuts, -0.22, 0.18)
    return jnp.clip(entries, -most, most).astype(held_as)


def setup_inputs(seed: int = 0) -> dict:
    key_list = jax.random.split(jax.random.key(seed), 8)
    return {
        "slide_tiles": scatter_about(key_list[0], (SLIDES, BLOCKS, P_SIZE, P_SIZE, C_IN), 1.0, 6.0, ((0, 8), (1, 32))),
        "balance_list": draw_balance_list(jax.random.fold_in(key_list[7], 71), 0),
        "output_grad": scatter_about(key_list[2], (SLIDES, BLOCKS, HALF, HALF, C_OUT), 1.0, 6.0, ((0, 8), (1, 32))),
        "w_reduce": scatter_about(key_list[3], (C_IN, C_MID), C_IN ** -0.5, 0.375),
        "w_spatial": scatter_about(key_list[4], (9 * C_MID, C_MID), (9 * C_MID) ** -0.5, 0.1875),
        "w_expand": scatter_about(key_list[5], (C_MID, C_OUT), C_MID ** -0.5, 0.5),
        "w_shortcut": scatter_about(key_list[6], (C_IN, C_OUT), C_IN ** -0.5, 0.375),
    }


def slope_silu(value):
    sig = jax.nn.sigmoid(value)
    return sig * (1.0 + value * (1.0 - sig))

def to_image(blocks, rows, cols):
    side = blocks.shape[1]
    depth = blocks.shape[3]
    shaped = blocks.reshape(rows, cols, side, side, depth)
    return shaped.transpose(0, 2, 1, 3, 4).reshape(rows * side, cols * side, depth)

def to_blocks(image, rows, cols, side):
    depth = image.shape[2]
    shaped = image.reshape(rows, side, cols, side, depth)
    return shaped.transpose(0, 2, 1, 3, 4).reshape(rows * cols, side, side, depth)

def conv_spatial(hidden, kernel):
    result = lax.conv_general_dilated(hidden[None], kernel, (2, 2), ((1, 1), (1, 1)), dimension_numbers=('NHWC', 'HWIO', 'NHWC'), precision=lax.Precision.HIGHEST)
    return result[0]

def one_slide(slide_blocks, balance, grad_blocks, w_reduce, w_spatial, w_expand, w_shortcut):
    rows = N_TILE
    cols = OWN
    tissue = balance >= 0
    inputs = jnp.where(tissue[:, None, None, None], slide_blocks, jnp.zeros((), slide_blocks.dtype))
    image = to_image(inputs, rows, cols)
    height = image.shape[0]
    width = image.shape[1]
    flat_in = image.reshape(-1, C_IN)
    pre = jnp.dot(flat_in, w_reduce, preferred_element_type=jnp.float32).reshape(height, width, C_MID)
    hidden = jax.nn.silu(pre).astype(jnp.bfloat16)
    kernel = w_spatial.astype(jnp.float32).reshape(3, 3, C_MID, C_MID)
    act = conv_spatial(hidden.astype(jnp.float32), kernel)
    gated = jax.nn.silu(act).astype(jnp.bfloat16)
    gated_flat = gated.reshape(-1, C_MID)
    skip_flat = image[::2, ::2].reshape(-1, C_IN)
    total = jnp.dot(gated_flat, w_expand, preferred_element_type=jnp.float32) + jnp.dot(skip_flat, w_shortcut, preferred_element_type=jnp.float32)
    out_mask = to_image(jnp.broadcast_to(tissue[:, None, None, None], (rows * cols, HALF, HALF, 1)), rows, cols).reshape(-1, 1)
    in_mask = to_image(jnp.broadcast_to(tissue[:, None, None, None], (rows * cols, P_SIZE, P_SIZE, 1)), rows, cols)
    grad_image = to_image(grad_blocks, rows, cols).reshape(-1, C_OUT)
    grad_total = jnp.where(out_mask, grad_image.astype(jnp.float32) * slope_silu(total), 0.0).astype(jnp.bfloat16)
    grad_expand = jnp.dot(gated_flat.T, grad_total, preferred_element_type=jnp.float32)
    grad_shortcut = jnp.dot(skip_flat.T, grad_total, preferred_element_type=jnp.float32)
    grad_gated = jnp.dot(grad_total, w_expand.T, preferred_element_type=jnp.float32).reshape(act.shape)
    grad_act = (grad_gated * slope_silu(act)).astype(jnp.bfloat16)
    unused, pullback = jax.vjp(conv_spatial, hidden.astype(jnp.float32), kernel)
    grad_hidden, grad_kernel = pullback(grad_act.astype(jnp.float32))
    grad_pre = jnp.where(in_mask, grad_hidden * slope_silu(pre), 0.0).astype(jnp.bfloat16)
    grad_pre_flat = grad_pre.reshape(-1, C_MID)
    grad_reduce = jnp.dot(flat_in.T, grad_pre_flat, preferred_element_type=jnp.float32)
    grad_input = jnp.dot(grad_pre_flat, w_reduce.T, preferred_element_type=jnp.float32).reshape(height, width, C_IN)
    skip_back = jnp.dot(grad_total, w_shortcut.T, preferred_element_type=jnp.float32).reshape(height // 2, width // 2, C_IN)
    grad_input = grad_input.at[::2, ::2].add(skip_back)
    grad_input = jnp.where(in_mask, grad_input, 0.0).astype(jnp.bfloat16)
    return (to_blocks(grad_input, rows, cols, P_SIZE), grad_reduce, grad_kernel.reshape(9 * C_MID, C_MID), grad_expand, grad_shortcut)

def reference(slide_tiles, balance_list, output_grad, w_reduce, w_spatial, w_expand, w_shortcut):

    def step(carry, inputs):
        slide_blocks, balance, grad_blocks = inputs
        grad_input, grad_reduce, grad_spatial, grad_expand, grad_shortcut = one_slide(slide_blocks, balance, grad_blocks, w_reduce, w_spatial, w_expand, w_shortcut)
        summed = (carry[0] + grad_reduce, carry[1] + grad_spatial, carry[2] + grad_expand, carry[3] + grad_shortcut)
        return (summed, grad_input)
    start = (jnp.zeros((C_IN, C_MID), jnp.float32), jnp.zeros((9 * C_MID, C_MID), jnp.float32), jnp.zeros((C_MID, C_OUT), jnp.float32), jnp.zeros((C_IN, C_OUT), jnp.float32))
    totals, input_grad = lax.scan(step, start, (slide_tiles, balance_list, output_grad))
    return (input_grad, totals[0], totals[1], totals[2], totals[3])
```

```python
import jax
import jax.numpy as jnp
from jax import lax
from jax.experimental import pallas as pl
from jax.experimental.pallas import tpu as pltpu
from jax.sharding import PartitionSpec as P

MESH = pl.DeviceIdType.MESH
F32 = jnp.float32
BF16 = jnp.bfloat16

ROWS = 16
OUT_ROWS = 8
WIDE = 512
HALF_WIDE = 256
MID = 128
N_XY = 16
N_Z = 8
CHUNK = 96
HALF_ROWS = N_XY * CHUNK


def nn(a, b):
    return lax.dot_general(a, b, (((1,), (0,)), ((), ())), preferred_element_type=F32)


def nt(a, b):
    return lax.dot_general(a, b, (((1,), (1,)), ((), ())), preferred_element_type=F32)


def tn(a, b):
    return lax.dot_general(a, b, (((0,), (0,)), ((), ())), preferred_element_type=F32)


def sigmoid(v):
    return 0.5 * jnp.tanh(0.5 * v) + 0.5


def kernel(
    x_hbm, bal_hbm, og_hbm, wr_hbm, wsp_hbm, we_hbm, wsc_hbm,
    ig_hbm, gr_out, gsp_out, gexp_out, gsc_out,
    xin, og, wr, wsp, we, wsc, bal,
    mask_in, mask_out, hid, dpre, even, odd, skip_f, skip, gated, gt, ga2, ga_f, wb,
    spread, gp, zskip, out_v, acc, core_in, xy_out, xy_in, z_in, done,
    x_sem, og_sem, w_sem, out_sem, halo_send, halo_recv,
    c_send, c_recv, xy_send, xy_recv, z_send, z_recv, b_send, b_recv, f_send, f_recv,
):
    s = lax.axis_index("slide")
    t = lax.axis_index("tile")
    y_lo = t // 16
    zi = (t // 2) % N_Z
    core = t % 2
    me = s * 2 + y_lo

    def xy_peer(q):
        return (q // 2, (q % 2) * 16 + t % 16)

    def z_peer(q):
        return (s, y_lo * 16 + q * 2 + core)

    core_peer = (s, t + 1 - 2 * core)
    down = (s, (t + 1) % 32)
    up = (s, (t + 31) % 32)

    def x_copy(y):
        return pltpu.make_async_copy(x_hbm.at[:, y], xin.at[y], x_sem.at[y])

    def og_copy(i):
        return pltpu.make_async_copy(og_hbm.at[:, i], og.at[i], og_sem.at[i])

    def out_copy(y):
        return pltpu.make_async_copy(out_v.at[y], ig_hbm.at[:, y], out_sem.at[y])

    w_copies = [
        pltpu.make_async_copy(a, b, w_sem.at[k])
        for k, (a, b) in enumerate(
            [(bal_hbm, bal), (wr_hbm, wr), (wsp_hbm, wsp), (we_hbm, we), (wsc_hbm, wsc)]
        )
    ]
    w_copies[0].start()
    w_copies[1].start()
    x_copy(14).start()
    x_copy(15).start()

    def start_x(y, c):
        x_copy(y).start()
        return c

    lax.fori_loop(0, ROWS - 2, start_x, 0)
    for copy in w_copies[2:]:
        copy.start()

    def start_og(i, c):
        og_copy(i).start()
        return c

    lax.fori_loop(0, OUT_ROWS, start_og, 0)

    barrier = pltpu.get_barrier_semaphore()

    def greet_xy(k, c):
        pl.semaphore_signal(barrier, 1, device_id=xy_peer((me + k) % N_XY), device_id_type=MESH)
        return c

    def greet_z(k, c):
        pl.semaphore_signal(barrier, 1, device_id=z_peer((zi + k) % N_Z), device_id_type=MESH)
        return c

    lax.fori_loop(1, N_XY, greet_xy, 0)
    lax.fori_loop(1, N_Z, greet_z, 0)
    for peer in (core_peer, down, up):
        pl.semaphore_signal(barrier, 1, device_id=peer, device_id_type=MESH)

    w_copies[0].wait()
    window = bal[:, pl.ds(pl.multiple_of((t // 4) * 128, 128), 128)]
    kept = jnp.broadcast_to(jnp.where(window >= 0, 1.0, 0.0).astype(F32), (128, 128)).astype(BF16)
    for ref, side in ((mask_in, 16), (mask_out, 8)):
        shape = ref.shape
        pixel = lax.broadcasted_iota(jnp.int32, shape, 0) // side
        lane = lax.broadcasted_iota(jnp.int32, shape, 1)
        chosen = jnp.where(lane == (t % 4) * 32 + pixel, 1.0, 0.0).astype(BF16)
        ref[...] = nt(chosen, kept)
    for slot in range(2):
        hid[slot, 0:8] = jnp.zeros((8, MID), F32)
    ga_f[HALF_WIDE : HALF_WIDE + 8] = jnp.zeros((8, MID), F32)
    acc[2944:3072] = jnp.zeros((128, 128), F32)
    zskip[...] = jnp.zeros(zskip.shape, F32)
    w_copies[1].wait()

    halo_down = pltpu.make_async_remote_copy(
        odd.at[8], odd.at[0], halo_send.at[0], halo_recv.at[0], device_id=down, device_id_type=MESH
    )
    halo_up = pltpu.make_async_remote_copy(
        ga2.at[0], ga2.at[8], halo_send.at[1], halo_recv.at[1], device_id=up, device_id_type=MESH
    )

    def hidden_pair(k, c):
        i = (k + 7) % 8
        for p in range(2):
            y = 2 * i + p
            x_copy(y).wait()
            pre = nn(xin[y].reshape(WIDE, 256), wr[...])
            sig = sigmoid(pre)
            h = pre * sig
            m = mask_in[...]
            dpre[y] = (sig + h * (1.0 - sig)) * m
            hid[p, 8 : 8 + WIDE] = h * m
            target = odd.at[i + 1] if p else even.at[i]
            for v in range(3):
                target[:, v * MID : (v + 1) * MID] = hid[p, pl.ds(7 + v, HALF_WIDE, stride=2)].astype(BF16)

        @pl.when(k == 0)
        def _():
            pl.semaphore_wait(barrier, N_XY - 1 + N_Z - 1 + 3)
            halo_down.start()

        return c

    lax.fori_loop(0, 8, hidden_pair, 0)

    for copy in w_copies[2:]:
        copy.wait()
    for u in range(3):
        tap = u * 3 * MID
        wb[u, 0:MID, 0:MID] = wsp[tap + MID : tap + 2 * MID]
        wb[u, 0:MID, MID:] = jnp.zeros((MID, MID), BF16)
        wb[u, MID:, 0:MID] = wsp[tap + 2 * MID : tap + 3 * MID]
        wb[u, MID:, MID:] = wsp[tap : tap + MID]

    def output_row(k, c):
        i = (k + 1) % 8

        @pl.when(k == 7)
        def _():
            halo_down.wait_recv()

            @pl.when(t == 0)
            def _():
                odd[0] = jnp.zeros(odd.shape[1:], BF16)

        act = nn(odd[i], wsp[0:384]) + nn(even[i], wsp[384:768]) + nn(odd[i + 1], wsp[768:1152])
        sig = sigmoid(act)
        h = act * sig
        dact = sig + h * (1.0 - sig)
        g = h.astype(BF16)
        gated[i] = g
        row = xin[2 * i].reshape(WIDE, 256).astype(F32)
        for half in range(2):
            skip_f[half] = row[:, half * 128 : (half + 1) * 128]
        for half in range(2):
            skip[i, :, half * 128 : (half + 1) * 128] = skip_f[half, pl.ds(0, HALF_WIDE, stride=2)].astype(BF16)
        total = nn(g, we[...]) + nn(skip[i], wsc[...])
        sig = sigmoid(total)
        slope = sig + total * sig * (1.0 - sig)
        og_copy(i).wait()
        m = mask_out[...]
        m = jnp.concatenate([m, m, m, m], axis=1)
        grad = og[i].astype(F32).reshape(HALF_WIDE, 512) * slope * m
        grad = grad.astype(BF16)
        gt[i] = grad
        ga = nt(grad, we[...]) * dact
        ga2[i, :, 0:MID] = ga.astype(BF16)
        ga_f[0:HALF_WIDE] = ga
        ga2[i, :, MID:] = ga_f[1 : 1 + HALF_WIDE].astype(BF16)
        return c

    lax.fori_loop(0, 8, output_row, 0)
    halo_up.start()

    gt_all = gt[...].reshape(8 * HALF_WIDE, 512)
    part = tn(skip[...].reshape(8 * HALF_WIDE, 256), gt_all)
    for k in range(4):
        acc[k * 256 : (k + 1) * 256] = part[:, k * 128 : (k + 1) * 128]
    part = tn(gated[...].reshape(8 * HALF_WIDE, MID), gt_all)
    for k in range(4):
        acc[1024 + k * 128 : 1152 + k * 128] = part[:, k * 128 : (k + 1) * 128]
    ga_all = ga2[0:8, :, 0:MID].reshape(8 * HALF_WIDE, MID)
    for u in range(3):
        taps = (odd[0:8], even[...], odd[1:9])[u].reshape(8 * HALF_WIDE, 384)
        part = tn(ga_all, taps)
        for v in range(3):
            at = 1536 + (u * 3 + v) * 128
            acc[at : at + 128] = part[:, v * 128 : (v + 1) * 128]

    def grad_pair(i, total):
        @pl.when(i == 7)
        def _():
            halo_up.wait_recv()

            @pl.when(t == 31)
            def _():
                ga2[8] = jnp.zeros(ga2.shape[1:], BF16)

        this = ga2[i]
        for p in range(2):
            y = 2 * i + p
            if p == 0:
                both = nt(this, wb[1])
            else:
                both = nt(this, wb[2]) + nt(ga2[i + 1], wb[0])
            spread[p, pl.ds(0, HALF_WIDE, stride=2)] = both[:, 0:MID]
            spread[p, pl.ds(1, HALF_WIDE, stride=2)] = both[:, MID:]
            g = (spread[p] * dpre[y]).astype(BF16)
            gp[y] = g
            total = total + tn(g, xin[y].reshape(WIDE, 256))
        return total

    part = lax.fori_loop(0, 8, grad_pair, jnp.zeros((MID, 256), F32))
    acc[2688:2816] = part[:, 0:128]
    acc[2816:2944] = part[:, 128:256]

    c_copies = []
    for k in range(4):
        rows = HALF_ROWS // 4
        c_copies.append(
            pltpu.make_async_remote_copy(
                acc.at[pl.ds(pl.multiple_of((1 - core) * HALF_ROWS + k * rows, 8), rows)],
                core_in.at[pl.ds(k * rows, rows)],
                c_send.at[k], c_recv.at[k], device_id=core_peer, device_id_type=MESH,
            )
        )
    for copy in c_copies:
        copy.start()

    def out_pair(i, c):
        back = nt(gt[i], wsc[...])
        for half in range(2):
            zskip[half, pl.ds(0, HALF_WIDE, stride=2)] = back[:, half * 128 : (half + 1) * 128]
        first = nt(gp[2 * i], wr[...]) + jnp.concatenate([zskip[0], zskip[1]], axis=1)
        out_v[2 * i] = first.astype(BF16).reshape(32, 16, 256)
        out_copy(2 * i).start()
        second = nt(gp[2 * i + 1], wr[...])
        out_v[2 * i + 1] = second.astype(BF16).reshape(32, 16, 256)
        out_copy(2 * i + 1).start()
        return c

    lax.fori_loop(0, 4, out_pair, 0)

    for copy in c_copies:
        copy.wait_recv()

    def xy_copy(q, slot):
        return pltpu.make_async_remote_copy(
            xy_out.at[q], xy_in.at[slot], xy_send.at[q], xy_recv.at[slot],
            device_id=xy_peer(q), device_id_type=MESH,
        )

    def both_cores(q):
        at = pl.multiple_of(q * CHUNK, 8)
        return acc[pl.ds(pl.multiple_of(core * HALF_ROWS + at, 8), CHUNK)] + core_in[pl.ds(at, CHUNK)]

    def send_xy(k, c):
        q = (me + k) % N_XY
        xy_out[q] = both_cores(q).astype(BF16)
        xy_copy(q, me).start()
        return c

    lax.fori_loop(1, N_XY, send_xy, 0)
    lax.fori_loop(4, 8, out_pair, 0)

    def take_xy(k, total):
        q = (me + k) % N_XY
        xy_copy(q, q).wait_recv()
        return total + xy_in[q].astype(F32)

    plane = lax.fori_loop(1, N_XY, take_xy, both_cores(me))

    z_in[zi] = plane.astype(BF16)

    def z_copy(q, slot):
        return pltpu.make_async_remote_copy(
            z_in.at[zi], z_in.at[slot], z_send.at[q], z_recv.at[slot],
            device_id=z_peer(q), device_id_type=MESH,
        )

    def send_z(k, c):
        z_copy((zi + k) % N_Z, zi).start()
        return c

    lax.fori_loop(1, N_Z, send_z, 0)

    def take_z(k, c):
        q = (zi + k) % N_Z
        z_copy(q, q).wait_recv()
        return c

    lax.fori_loop(1, N_Z, take_z, 0)
    whole = z_in[0].astype(F32)
    for q in range(1, N_Z):
        whole = whole + z_in[q].astype(F32)

    mine = core * N_XY
    done[mine + me] = whole.astype(BF16)

    def back_copy(q, slot):
        return pltpu.make_async_remote_copy(
            done.at[mine + me], done.at[mine + slot], b_send.at[q], b_recv.at[slot],
            device_id=xy_peer(q), device_id_type=MESH,
        )

    def pass_copy(q, side):
        return pltpu.make_async_remote_copy(
            done.at[mine + q], done.at[side * N_XY + q], f_send.at[q], f_recv.at[q],
            device_id=core_peer, device_id_type=MESH,
        )

    def send_back(k, c):
        back_copy((me + k) % N_XY, me).start()
        return c

    lax.fori_loop(1, N_XY, send_back, 0)
    pass_copy(me, core).start()

    def pass_on(k, c):
        q = (me + k) % N_XY
        back_copy(q, q).wait_recv()
        pass_copy(q, core).start()
        return c

    lax.fori_loop(1, N_XY, pass_on, 0)

    def take_passed(q, c):
        pass_copy(q, 1 - core).wait_recv()
        return c

    lax.fori_loop(0, N_XY, take_passed, 0)

    packed = done[...].astype(F32).reshape(2 * HALF_ROWS, 128)
    for k in range(4):
        gsc_out[:, k * 128 : (k + 1) * 128] = packed[k * 256 : (k + 1) * 256]
        gexp_out[:, k * 128 : (k + 1) * 128] = packed[1024 + k * 128 : 1152 + k * 128]
    for k in range(9):
        gsp_out[k * 128 : (k + 1) * 128] = packed[1536 + k * 128 : 1664 + k * 128].T
    for k in range(2):
        gr_out[k * 128 : (k + 1) * 128] = packed[2688 + k * 128 : 2816 + k * 128].T

    halo_down.wait_send()
    halo_up.wait_send()
    for copy in c_copies:
        copy.wait_send()

    def sent_xy(k, c):
        q = (me + k) % N_XY
        xy_copy(q, me).wait_send()
        back_copy(q, me).wait_send()
        return c

    lax.fori_loop(1, N_XY, sent_xy, 0)

    def sent_z(k, c):
        z_copy((zi + k) % N_Z, zi).wait_send()
        return c

    lax.fori_loop(1, N_Z, sent_z, 0)

    def sent_pass(q, c):
        pass_copy(q, core).wait_send()
        return c

    lax.fori_loop(0, N_XY, sent_pass, 0)

    def written(y, c):
        out_copy(y).wait()
        return c

    lax.fori_loop(0, ROWS, written, 0)


def body(slide_tiles, balance_list, output_grad, w_reduce, w_spatial, w_expand, w_shortcut):
    dma = pltpu.SemaphoreType.DMA
    any_spec = pl.BlockSpec(memory_space=pl.ANY)
    vmem_spec = pl.BlockSpec(memory_space=pltpu.VMEM)
    out = pl.pallas_call(
        kernel,
        out_shape=(
            jax.ShapeDtypeStruct((32, 16, 16, 256), BF16),
            jax.ShapeDtypeStruct((256, 128), F32),
            jax.ShapeDtypeStruct((1152, 128), F32),
            jax.ShapeDtypeStruct((128, 512), F32),
            jax.ShapeDtypeStruct((256, 512), F32),
        ),
        in_specs=[any_spec] * 7,
        out_specs=(any_spec, vmem_spec, vmem_spec, vmem_spec, vmem_spec),
        scratch_shapes=[
            pltpu.VMEM((16, 32, 16, 256), BF16),
            pltpu.VMEM((8, 32, 8, 512), BF16),
            pltpu.VMEM((256, 128), BF16),
            pltpu.VMEM((1152, 128), BF16),
            pltpu.VMEM((128, 512), BF16),
            pltpu.VMEM((256, 512), BF16),
            pltpu.VMEM((1, 1024), jnp.int32),
            pltpu.VMEM((WIDE, 128), F32),
            pltpu.VMEM((HALF_WIDE, 128), F32),
            pltpu.VMEM((2, WIDE + 16, MID), F32),
            pltpu.VMEM((16, WIDE, MID), F32),
            pltpu.VMEM((8, HALF_WIDE, 384), BF16),
            pltpu.VMEM((9, HALF_WIDE, 384), BF16),
            pltpu.VMEM((2, WIDE, 128), F32),
            pltpu.VMEM((8, HALF_WIDE, 256), BF16),
            pltpu.VMEM((8, HALF_WIDE, MID), BF16),
            pltpu.VMEM((8, HALF_WIDE, 512), BF16),
            pltpu.VMEM((9, HALF_WIDE, 256), BF16),
            pltpu.VMEM((HALF_WIDE + 8, MID), F32),
            pltpu.VMEM((3, 256, 256), BF16),
            pltpu.VMEM((2, WIDE, MID), F32),
            pltpu.VMEM((16, WIDE, MID), BF16),
            pltpu.VMEM((2, WIDE, 128), F32),
            pltpu.VMEM((16, 32, 16, 256), BF16),
            pltpu.VMEM((2 * HALF_ROWS, 128), F32),
            pltpu.VMEM((HALF_ROWS, 128), F32),
            pltpu.VMEM((N_XY, CHUNK, 128), BF16),
            pltpu.VMEM((N_XY, CHUNK, 128), BF16),
            pltpu.VMEM((N_Z, CHUNK, 128), BF16),
            pltpu.VMEM((2 * N_XY, CHUNK, 128), BF16),
            dma((16,)),
            dma((8,)),
            dma((5,)),
            dma((16,)),
            dma((2,)),
            dma((2,)),
            dma((4,)),
            dma((4,)),
            dma((N_XY,)),
            dma((N_XY,)),
            dma((N_Z,)),
            dma((N_Z,)),
            dma((N_XY,)),
            dma((N_XY,)),
            dma((N_XY,)),
            dma((N_XY,)),
        ],
        compiler_params=pltpu.CompilerParams(
            collective_id=0, has_side_effects=True, vmem_limit_bytes=56 * 2**20
        ),
    )(slide_tiles[0], balance_list, output_grad[0], w_reduce, w_spatial, w_expand, w_shortcut)
    return (out[0][None], out[1], out[2], out[3], out[4])


def solution(mesh):
    in_specs = (
        P("slide", "tile", None, None, None),
        P("slide", None),
        P("slide", "tile", None, None, None),
        P(),
        P(),
        P(),
        P(),
    )
    out_specs = (P("slide", "tile", None, None, None), P(), P(), P(), P())
    return jax.shard_map(body, mesh=mesh, in_specs=in_specs, out_specs=out_specs, check_vma=False)
```

```python
import jax
import jax.numpy as jnp
from jax import lax
from jax.experimental import pallas as pl
from jax.experimental.pallas import tpu as pltpu
from jax.sharding import PartitionSpec as P

MESH = pl.DeviceIdType.MESH
F32 = jnp.float32
BF16 = jnp.bfloat16

ROWS = 16
OUT_ROWS = 8
WIDE = 512
HALF_WIDE = 256
MID = 128
N_XY = 16
N_Z = 8
CHUNKS = (80, 16)
CHUNK = 96
SHARE = 12


def nn(a, b):
    return lax.dot_general(a, b, (((1,), (0,)), ((), ())), preferred_element_type=F32)


def nt(a, b):
    return lax.dot_general(a, b, (((1,), (1,)), ((), ())), preferred_element_type=F32)


def tn(a, b):
    return lax.dot_general(a, b, (((0,), (0,)), ((), ())), preferred_element_type=F32)


def silu_parts(half, scale=None):
    u = jnp.tanh(half)
    twice = 1.0 + u
    if scale is not None:
        twice = twice * scale
    h = half * twice
    return h, twice + h * (1.0 - u)


def kernel(
    x_hbm, bal_hbm, og_hbm, wr_hbm, wsp_hbm, we_hbm, wsc_hbm,
    out_v, done,
    xin, og, wr, wsp, we, wsc, bal,
    mask_in, mask_out, hid, dpre, even, odd, skip_f, skip, gated, gt, ga2, ga_f, wb,
    spread, gp, zskip, wr_h, wsp_h, we_h, wsc_h,
    acc_a, acc_b, core_a, core_b, xy_out_a, xy_out_b, xy_in_a, xy_in_b, plane_f, z_out, z_in, z_done,
    x_sem, og_sem, w_sem, halo_send, halo_recv,
    c_send, c_recv, xy_send_a, xy_send_b, xy_recv_a, xy_recv_b, z_send, z_recv, g_send, g_recv,
    b_send, b_recv, f_send, f_recv,
):
    s = lax.axis_index("slide")
    t = lax.axis_index("tile")
    y_lo = t // 16
    zi = (t // 2) % N_Z
    core = t % 2
    me = s * 2 + y_lo

    def xy_peer(q):
        return (q // 2, (q % 2) * 16 + t % 16)

    def z_peer(q):
        return (s, y_lo * 16 + q * 2 + core)

    core_peer = (s, t + 1 - 2 * core)
    down = (s, (t + 1) % 32)
    up = (s, (t + 31) % 32)

    def x_copy(y):
        return pltpu.make_async_copy(x_hbm.at[:, y], xin.at[y], x_sem.at[y])

    def og_copy(i):
        return pltpu.make_async_copy(og_hbm.at[:, i], og.at[i], og_sem.at[i])

    w_copies = [
        pltpu.make_async_copy(a, b, w_sem.at[k])
        for k, (a, b) in enumerate(
            [(bal_hbm, bal), (wr_hbm, wr), (wsp_hbm, wsp), (we_hbm, we), (wsc_hbm, wsc)]
        )
    ]
    w_copies[0].start()
    w_copies[1].start()
    x_copy(14).start()
    x_copy(15).start()

    def start_x(y, c):
        x_copy(y).start()
        return c

    lax.fori_loop(0, ROWS - 2, start_x, 0)
    for copy in w_copies[2:]:
        copy.start()

    def start_og(i, c):
        og_copy(i).start()
        return c

    lax.fori_loop(0, OUT_ROWS, start_og, 0)

    barrier = pltpu.get_barrier_semaphore()

    def greet_xy(k, c):
        pl.semaphore_signal(barrier, 1, device_id=xy_peer((me + k) % N_XY), device_id_type=MESH)
        return c

    def greet_z(k, c):
        pl.semaphore_signal(barrier, 1, device_id=z_peer((zi + k) % N_Z), device_id_type=MESH)
        return c

    lax.fori_loop(1, N_XY, greet_xy, 0)
    lax.fori_loop(1, N_Z, greet_z, 0)
    for peer in (core_peer, down, up):
        pl.semaphore_signal(barrier, 1, device_id=peer, device_id_type=MESH)

    w_copies[0].wait()
    window = bal[:, pl.ds(pl.multiple_of((t // 4) * 128, 128), 128)]
    kept = jnp.broadcast_to(jnp.where(window >= 0, 1.0, 0.0).astype(F32), (128, 128)).astype(BF16)
    for ref, side, scale in ((mask_in, 16, 1.0), (mask_out, 8, 0.5)):
        shape = ref.shape
        pixel = lax.broadcasted_iota(jnp.int32, shape, 0) // side
        lane = lax.broadcasted_iota(jnp.int32, shape, 1)
        chosen = jnp.where(lane == (t % 4) * 32 + pixel, 1.0, 0.0).astype(BF16)
        ref[...] = nt(chosen, kept) * scale
    for slot in range(2):
        hid[slot, 0:8] = jnp.zeros((8, MID), F32)
    ga_f[HALF_WIDE : HALF_WIDE + 8] = jnp.zeros((8, MID), F32)
    acc_b[384:512] = jnp.zeros((128, 128), F32)
    zskip[...] = jnp.zeros(zskip.shape, F32)
    w_copies[1].wait()
    wr_h[...] = wr[...] * jnp.asarray(0.5, BF16)

    halo_down = pltpu.make_async_remote_copy(
        odd.at[8], odd.at[0], halo_send.at[0], halo_recv.at[0], device_id=down, device_id_type=MESH
    )
    halo_up = pltpu.make_async_remote_copy(
        ga2.at[0], ga2.at[8], halo_send.at[1], halo_recv.at[1], device_id=up, device_id_type=MESH
    )

    def hidden_pair(k, c):
        i = (k + 7) % 8
        for p in range(2):
            y = 2 * i + p
            x_copy(y).wait()
            h, slope = silu_parts(nn(xin[y].reshape(WIDE, 256), wr_h[...]), mask_in[...])
            dpre[y] = slope
            hid[p, 8 : 8 + WIDE] = h
            target = odd.at[i + 1] if p else even.at[i]
            for v in range(3):
                target[:, v * MID : (v + 1) * MID] = hid[p, pl.ds(7 + v, HALF_WIDE, stride=2)].astype(BF16)

        return c

    lax.fori_loop(0, 8, hidden_pair, 0)
    pl.semaphore_wait(barrier, N_XY - 1 + N_Z - 1 + 3)
    halo_down.start()

    for copy in w_copies[2:]:
        copy.wait()
    for to, of in ((wsp_h, wsp), (we_h, we), (wsc_h, wsc)):
        to[...] = of[...] * jnp.asarray(0.5, BF16)
    for u in range(3):
        tap = u * 3 * MID
        wb[u, 0:MID, 0:MID] = wsp_h[tap + MID : tap + 2 * MID]
        wb[u, 0:MID, MID:] = jnp.zeros((MID, MID), BF16)
        wb[u, MID:, 0:MID] = wsp_h[tap + 2 * MID : tap + 3 * MID]
        wb[u, MID:, MID:] = wsp_h[tap : tap + MID]

    def output_row(k, c):
        i = (k + 1) % 8

        @pl.when(k == 7)
        def _():
            halo_down.wait_recv()

            @pl.when(t == 0)
            def _():
                odd[0] = jnp.zeros(odd.shape[1:], BF16)

        half = nn(odd[i], wsp_h[0:384]) + nn(even[i], wsp_h[384:768]) + nn(odd[i + 1], wsp_h[768:1152])
        h, dact = silu_parts(half)
        g = h.astype(BF16)
        gated[i] = g
        row = xin[2 * i].reshape(WIDE, 256).astype(F32)
        for half in range(2):
            skip_f[half] = row[:, half * 128 : (half + 1) * 128]
        for half in range(2):
            skip[i, :, half * 128 : (half + 1) * 128] = skip_f[half, pl.ds(0, HALF_WIDE, stride=2)].astype(BF16)
        half = nn(g, we_h[...]) + nn(skip[i], wsc_h[...])
        og_copy(i).wait()
        m = mask_out[...]
        m = jnp.concatenate([m, m, m, m], axis=1)
        _, slope = silu_parts(half, m)
        grad = (og[i].astype(F32).reshape(HALF_WIDE, 512) * slope).astype(BF16)
        gt[i] = grad
        ga = nt(grad, we_h[...]) * dact
        ga2[i, :, 0:MID] = ga.astype(BF16)
        ga_f[0:HALF_WIDE] = ga
        ga2[i, :, MID:] = ga_f[1 : 1 + HALF_WIDE].astype(BF16)
        return c

    lax.fori_loop(0, 8, output_row, 0)
    halo_up.start()

    gt_all = gt[...].reshape(8 * HALF_WIDE, 512)
    part = tn(skip[...].reshape(8 * HALF_WIDE, 256), gt_all)
    for k in range(4):
        acc_a[k * 256 : (k + 1) * 256] = part[:, k * 128 : (k + 1) * 128]
    part = tn(gated[...].reshape(8 * HALF_WIDE, MID), gt_all)
    for k in range(4):
        acc_a[1024 + k * 128 : 1152 + k * 128] = part[:, k * 128 : (k + 1) * 128]
    ga_all = ga2[0:8, :, 0:MID].reshape(8 * HALF_WIDE, MID)
    for u in range(3):
        taps = (odd[0:8], even[...], odd[1:9])[u].reshape(8 * HALF_WIDE, 384)
        part = tn(ga_all, taps)
        for v in range(3):
            tap = u * 3 + v
            to, at = (acc_a, 1536 + tap * 128) if tap < 8 else (acc_b, 0)
            to[at : at + 128] = part[:, v * 128 : (v + 1) * 128]

    def grad_pair(i, total):
        @pl.when(i == 7)
        def _():
            halo_up.wait_recv()

            @pl.when(t == 31)
            def _():
                ga2[8] = jnp.zeros(ga2.shape[1:], BF16)

        this = ga2[i]
        for p in range(2):
            y = 2 * i + p
            if p == 0:
                both = nt(this, wb[1])
            else:
                both = nt(this, wb[2]) + nt(ga2[i + 1], wb[0])
            spread[p, pl.ds(0, HALF_WIDE, stride=2)] = both[:, 0:MID]
            spread[p, pl.ds(1, HALF_WIDE, stride=2)] = both[:, MID:]
            g = (spread[p] * dpre[y]).astype(BF16)
            gp[y] = g
            total = total + tn(g, xin[y].reshape(WIDE, 256))
        return total

    def out_pair(i, c):
        back = nt(gt[i], wsc[...])
        for half in range(2):
            zskip[half, pl.ds(0, HALF_WIDE, stride=2)] = back[:, half * 128 : (half + 1) * 128]
        first = nt(gp[2 * i], wr[...]) + jnp.concatenate([zskip[0], zskip[1]], axis=1)
        out_v[2 * i] = first.astype(BF16).reshape(32, 16, 256)
        second = nt(gp[2 * i + 1], wr[...])
        out_v[2 * i + 1] = second.astype(BF16).reshape(32, 16, 256)
        return c

    accs, cores = (acc_a, acc_b), (core_a, core_b)
    xy_outs, xy_ins = (xy_out_a, xy_out_b), (xy_in_a, xy_in_b)
    xy_sends, xy_recvs = (xy_send_a, xy_send_b), (xy_recv_a, xy_recv_b)

    def core_copy(part):
        rows = N_XY * CHUNKS[part]
        return pltpu.make_async_remote_copy(
            accs[part].at[pl.ds(pl.multiple_of((1 - core) * rows, 8), rows)], cores[part],
            c_send.at[part], c_recv.at[part], device_id=core_peer, device_id_type=MESH,
        )

    def xy_copy(part, q, slot):
        return pltpu.make_async_remote_copy(
            xy_outs[part].at[q], xy_ins[part].at[slot], xy_sends[part].at[q], xy_recvs[part].at[slot],
            device_id=xy_peer(q), device_id_type=MESH,
        )

    def both_cores(part, q):
        chunk = CHUNKS[part]
        at = pl.multiple_of(q * chunk, 8)
        kept = accs[part][pl.ds(pl.multiple_of(core * (N_XY * chunk) + at, 8), chunk)]
        return kept + cores[part][pl.ds(at, chunk)]

    def send_xy(part):
        def step(k, c):
            q = (me + k) % N_XY
            xy_outs[part][q] = both_cores(part, q).astype(BF16)
            xy_copy(part, q, me).start()
            return c

        lax.fori_loop(1, N_XY, step, 0)

    def take_xy(part):
        def step(k, total):
            q = (me + N_XY - k) % N_XY
            xy_copy(part, q, q).wait_recv()
            return total + xy_ins[part][q].astype(F32)

        return lax.fori_loop(1, N_XY, step, both_cores(part, me))

    def z_copy(q, slot):
        return pltpu.make_async_remote_copy(
            z_out.at[q], z_in.at[slot], z_send.at[q], z_recv.at[slot],
            device_id=z_peer(q), device_id_type=MESH,
        )

    def share_copy(q, slot):
        return pltpu.make_async_remote_copy(
            z_done.at[zi], z_done.at[slot], g_send.at[q], g_recv.at[slot],
            device_id=z_peer(q), device_id_type=MESH,
        )

    def send_z(k, c):
        z_copy((zi + k) % N_Z, zi).start()
        return c

    def take_z(k, c):
        q = (zi + N_Z - k) % N_Z
        z_copy(q, q).wait_recv()
        return c

    def send_share(k, c):
        share_copy((zi + k) % N_Z, zi).start()
        return c

    def take_share(k, c):
        q = (zi + N_Z - k) % N_Z
        share_copy(q, q).wait_recv()
        return c

    mine = core * N_XY

    def back_copy(q, slot):
        return pltpu.make_async_remote_copy(
            done.at[mine + me], done.at[mine + slot], b_send.at[q], b_recv.at[slot],
            device_id=xy_peer(q), device_id_type=MESH,
        )

    def pass_copy(q, side):
        return pltpu.make_async_remote_copy(
            done.at[mine + q], done.at[side * N_XY + q], f_send.at[q], f_recv.at[q],
            device_id=core_peer, device_id_type=MESH,
        )

    def send_back(k, c):
        back_copy((me + k) % N_XY, me).start()
        return c

    def pass_on(k, c):
        q = (me + N_XY - k) % N_XY
        back_copy(q, q).wait_recv()
        pass_copy(q, core).start()
        return c

    def take_passed(k, c):
        pass_copy((me + N_XY - k) % N_XY, 1 - core).wait_recv()
        return c

    core_copy(0).start()
    total = lax.fori_loop(0, 2, grad_pair, jnp.zeros((MID, 256), F32))
    core_copy(0).wait_recv()
    send_xy(0)
    total = lax.fori_loop(2, 8, grad_pair, total)
    acc_b[128:256] = total[:, 0:128]
    acc_b[256:384] = total[:, 128:256]
    core_copy(1).start()
    lax.fori_loop(0, 3, out_pair, 0)
    core_copy(1).wait_recv()
    send_xy(1)
    lax.fori_loop(3, 6, out_pair, 0)
    plane_f[0:80] = take_xy(0)
    plane_f[80:96] = take_xy(1)
    for q in range(N_Z):
        z_out[q, 0:SHARE] = plane_f[q * SHARE : (q + 1) * SHARE].astype(BF16)
    z_in[zi] = z_out[zi]
    lax.fori_loop(1, N_Z, send_z, 0)
    lax.fori_loop(6, 7, out_pair, 0)
    lax.fori_loop(1, N_Z, take_z, 0)
    share = z_in[0, 0:SHARE].astype(F32)
    for q in range(1, N_Z):
        share = share + z_in[q, 0:SHARE].astype(F32)
    z_done[zi, 0:SHARE] = share.astype(BF16)
    lax.fori_loop(1, N_Z, send_share, 0)
    lax.fori_loop(7, 8, out_pair, 0)
    lax.fori_loop(1, N_Z, take_share, 0)
    for q in range(N_Z):
        plane_f[q * SHARE : (q + 1) * SHARE] = z_done[q, 0:SHARE].astype(F32)
    done[mine + me] = plane_f[...].astype(BF16)
    lax.fori_loop(1, N_XY, send_back, 0)
    pass_copy(me, core).start()
    lax.fori_loop(1, N_XY, pass_on, 0)
    lax.fori_loop(0, N_XY, take_passed, 0)

    halo_down.wait_send()
    halo_up.wait_send()
    for part in range(2):
        core_copy(part).wait_send()

    def sent_xy(k, c):
        q = (me + k) % N_XY
        for part in range(2):
            xy_copy(part, q, me).wait_send()
        back_copy(q, me).wait_send()
        return c

    lax.fori_loop(1, N_XY, sent_xy, 0)

    def sent_z(k, c):
        q = (zi + k) % N_Z
        z_copy(q, zi).wait_send()
        share_copy(q, zi).wait_send()
        return c

    lax.fori_loop(1, N_Z, sent_z, 0)

    def sent_pass(q, c):
        pass_copy(q, core).wait_send()
        return c

    lax.fori_loop(0, N_XY, sent_pass, 0)


def write_out(
    out_v, done, ig_hbm, gr_hbm, gsp_hbm, gexp_hbm, gsc_hbm, gr, gsp, gexp, gsc, out_sem, w_sem
):
    copies = [
        pltpu.make_async_copy(out_v.at[y], ig_hbm.at[:, y], out_sem.at[y]) for y in range(ROWS)
    ]
    for copy in copies:
        copy.start()
    part = done[:, 0:80].astype(F32).reshape(2560, 128)
    last = done[:, 80:96].astype(F32).reshape(512, 128)
    for k in range(4):
        gsc[:, k * 128 : (k + 1) * 128] = part[k * 256 : (k + 1) * 256]
        gexp[:, k * 128 : (k + 1) * 128] = part[1024 + k * 128 : 1152 + k * 128]
    for k in range(8):
        gsp[k * 128 : (k + 1) * 128] = part[1536 + k * 128 : 1664 + k * 128].T
    gsp[1024:1152] = last[0:128].T
    for k in range(2):
        gr[k * 128 : (k + 1) * 128] = last[128 + k * 128 : 256 + k * 128].T
    pairs = ((gr, gr_hbm), (gsp, gsp_hbm), (gexp, gexp_hbm), (gsc, gsc_hbm))
    more = [pltpu.make_async_copy(a, b, w_sem.at[k]) for k, (a, b) in enumerate(pairs)]
    for copy in more:
        copy.start()
    for copy in copies + more:
        copy.wait()


def body(slide_tiles, balance_list, output_grad, w_reduce, w_spatial, w_expand, w_shortcut):
    dma = pltpu.SemaphoreType.DMA
    any_spec = pl.BlockSpec(memory_space=pltpu.HBM)
    vmem_spec = pl.BlockSpec(memory_space=pltpu.VMEM)
    out_v, done = pl.pallas_call(
        kernel,
        out_shape=(
            pltpu.VMEM((16, 32, 16, 256), BF16),
            pltpu.VMEM((2 * N_XY, CHUNK, 128), BF16),
        ),
        in_specs=[any_spec] * 7,
        out_specs=(vmem_spec, vmem_spec),
        scratch_shapes=[
            pltpu.VMEM((16, 32, 16, 256), BF16),
            pltpu.VMEM((8, 32, 8, 512), BF16),
            pltpu.VMEM((256, 128), BF16),
            pltpu.VMEM((1152, 128), BF16),
            pltpu.VMEM((128, 512), BF16),
            pltpu.VMEM((256, 512), BF16),
            pltpu.VMEM((1, 1024), jnp.int32),
            pltpu.VMEM((WIDE, 128), F32),
            pltpu.VMEM((HALF_WIDE, 128), F32),
            pltpu.VMEM((2, WIDE + 16, MID), F32),
            pltpu.VMEM((16, WIDE, MID), F32),
            pltpu.VMEM((8, HALF_WIDE, 384), BF16),
            pltpu.VMEM((9, HALF_WIDE, 384), BF16),
            pltpu.VMEM((2, WIDE, 128), F32),
            pltpu.VMEM((8, HALF_WIDE, 256), BF16),
            pltpu.VMEM((8, HALF_WIDE, MID), BF16),
            pltpu.VMEM((8, HALF_WIDE, 512), BF16),
            pltpu.VMEM((9, HALF_WIDE, 256), BF16),
            pltpu.VMEM((HALF_WIDE + 8, MID), F32),
            pltpu.VMEM((3, 256, 256), BF16),
            pltpu.VMEM((2, WIDE, MID), F32),
            pltpu.VMEM((16, WIDE, MID), BF16),
            pltpu.VMEM((2, WIDE, 128), F32),
            pltpu.VMEM((256, 128), BF16),
            pltpu.VMEM((1152, 128), BF16),
            pltpu.VMEM((128, 512), BF16),
            pltpu.VMEM((256, 512), BF16),
            pltpu.VMEM((2560, 128), F32),
            pltpu.VMEM((512, 128), F32),
            pltpu.VMEM((1280, 128), F32),
            pltpu.VMEM((256, 128), F32),
            pltpu.VMEM((N_XY, 80, 128), BF16),
            pltpu.VMEM((N_XY, 16, 128), BF16),
            pltpu.VMEM((N_XY, 80, 128), BF16),
            pltpu.VMEM((N_XY, 16, 128), BF16),
            pltpu.VMEM((CHUNK, 128), F32),
            pltpu.VMEM((N_Z, 16, 128), BF16),
            pltpu.VMEM((N_Z, 16, 128), BF16),
            pltpu.VMEM((N_Z, 16, 128), BF16),
            dma((16,)),
            dma((8,)),
            dma((5,)),
            dma((2,)),
            dma((2,)),
            dma((2,)),
            dma((2,)),
            dma((N_XY,)),
            dma((N_XY,)),
            dma((N_XY,)),
            dma((N_XY,)),
            dma((N_Z,)),
            dma((N_Z,)),
            dma((N_Z,)),
            dma((N_Z,)),
            dma((N_XY,)),
            dma((N_XY,)),
            dma((N_XY,)),
            dma((N_XY,)),
        ],
        compiler_params=pltpu.CompilerParams(
            collective_id=0, has_side_effects=True, vmem_limit_bytes=59 * 2**20
        ),
    )(slide_tiles[0], balance_list, output_grad[0], w_reduce, w_spatial, w_expand, w_shortcut)
    shapes = ((256, 128), (1152, 128), (128, 512), (256, 512))
    out = pl.pallas_call(
        write_out,
        out_shape=[jax.ShapeDtypeStruct((32, 16, 16, 256), BF16)]
        + [jax.ShapeDtypeStruct(shape, F32) for shape in shapes],
        in_specs=[vmem_spec, vmem_spec],
        out_specs=[any_spec] * 5,
        scratch_shapes=[pltpu.VMEM(shape, F32) for shape in shapes] + [dma((16,)), dma((4,))],
        compiler_params=pltpu.CompilerParams(vmem_limit_bytes=16 * 2**20),
    )(out_v, done)
    return (out[0][None], out[1], out[2], out[3], out[4])


def solution(mesh):
    in_specs = (
        P("slide", "tile", None, None, None),
        P("slide", None),
        P("slide", "tile", None, None, None),
        P(),
        P(),
        P(),
        P(),
    )
    out_specs = (P("slide", "tile", None, None, None), P(), P(), P(), P())
    return jax.shard_map(body, mesh=mesh, in_specs=in_specs, out_specs=out_specs, check_vma=False)
```

```python
import jax
import jax.numpy as jnp
from jax import lax
from jax.experimental import pallas as pl
from jax.experimental.pallas import tpu as pltpu
from jax.sharding import PartitionSpec as P

MESH = pl.DeviceIdType.MESH
F32 = jnp.float32
BF16 = jnp.bfloat16

ROWS = 16
OUT_ROWS = 8
WIDE = 512
HALF_WIDE = 256
MID = 128
N_XY = 16
N_Z = 8
CHUNKS = (80, 16)


def nn(a, b):
    return lax.dot_general(a, b, (((1,), (0,)), ((), ())), preferred_element_type=F32)


def nt(a, b):
    return lax.dot_general(a, b, (((1,), (1,)), ((), ())), preferred_element_type=F32)


def tn(a, b):
    return lax.dot_general(a, b, (((0,), (0,)), ((), ())), preferred_element_type=F32)


def silu_parts(half, scale=None):
    u = jnp.tanh(half)
    twice = 1.0 + u
    if scale is not None:
        twice = twice * scale
    h = half * twice
    return h, twice + h * (1.0 - u)


def kernel(
    x_hbm, bal_hbm, og_hbm, wr_hbm, wsp_hbm, we_hbm, wsc_hbm,
    out_v, done_a, done_b,
    xin, og, wr, wsp, we, wsc, bal,
    mask_in, mask_out, hid, dpre, even, odd, skip_fs, skip, gated, gt, ga2, ga_fs, wb, dacts,
    spreads, gp, zskips, wr_h, wsp_h, we_h, wsc_h,
    acc_a, acc_b, core_a, core_b, xy_out_a, xy_out_b, xy_in_a, xy_in_b, z_in_a, z_in_b,
    x_sem, og_sem, w_sem, halo_send, halo_recv,
    c_send, c_recv, xy_send_a, xy_send_b, xy_recv_a, xy_recv_b,
    z_send_a, z_send_b, z_recv_a, z_recv_b, b_send_a, b_send_b, b_recv_a, b_recv_b,
    f_send_a, f_send_b, f_recv_a, f_recv_b,
):
    s = lax.axis_index("slide")
    t = lax.axis_index("tile")
    y_lo = t // 16
    zi = (t // 2) % N_Z
    core = t % 2
    me = s * 2 + y_lo

    def xy_peer(q):
        return (q // 2, (q % 2) * 16 + t % 16)

    def z_peer(q):
        return (s, y_lo * 16 + q * 2 + core)

    x, y = me // 4, me % 4
    steps = sorted(((a, b) for a in range(4) for b in range(4) if a or b), key=lambda d: -min(d[0], 4 - d[0]) - min(d[1], 4 - d[1]))
    xy_to = [(x + a) % 4 * 4 + (y + b) % 4 for a, b in steps]
    xy_from = [(x + 4 - a) % 4 * 4 + (y + 4 - b) % 4 for a, b in steps]
    z_to = [(zi + k) % N_Z for k in (4, 3, 5, 2, 6, 1, 7)]
    z_from = [(zi + N_Z - k) % N_Z for k in (4, 3, 5, 2, 6, 1, 7)]

    core_peer = (s, t + 1 - 2 * core)
    down = (s, (t + 1) % 32)
    up = (s, (t + 31) % 32)

    def x_copy(y):
        return pltpu.make_async_copy(x_hbm.at[:, y], xin.at[y], x_sem.at[y])

    def og_copy(i):
        return pltpu.make_async_copy(og_hbm.at[:, i], og.at[i], og_sem.at[i])

    w_copies = [
        pltpu.make_async_copy(a, b, w_sem.at[k])
        for k, (a, b) in enumerate(
            [(bal_hbm, bal), (wr_hbm, wr), (wsp_hbm, wsp), (we_hbm, we), (wsc_hbm, wsc)]
        )
    ]
    w_copies[0].start()
    w_copies[1].start()
    x_copy(14).start()
    x_copy(15).start()

    def start_x(y, c):
        x_copy(y).start()
        return c

    lax.fori_loop(0, ROWS - 2, start_x, 0)
    for copy in w_copies[2:]:
        copy.start()

    def start_og(i, c):
        og_copy(i).start()
        return c

    lax.fori_loop(0, OUT_ROWS, start_og, 0)

    barrier = pltpu.get_barrier_semaphore()

    def greet_xy(k, c):
        pl.semaphore_signal(barrier, 1, device_id=xy_peer((me + k) % N_XY), device_id_type=MESH)
        return c

    def greet_z(k, c):
        pl.semaphore_signal(barrier, 1, device_id=z_peer((zi + k) % N_Z), device_id_type=MESH)
        return c

    lax.fori_loop(1, N_XY, greet_xy, 0)
    lax.fori_loop(1, N_Z, greet_z, 0)
    for peer in (core_peer, down, up):
        pl.semaphore_signal(barrier, 1, device_id=peer, device_id_type=MESH)

    w_copies[0].wait()
    window = bal[:, pl.ds(pl.multiple_of((t // 4) * 128, 128), 128)]
    kept = jnp.broadcast_to(jnp.where(window >= 0, 1.0, 0.0).astype(F32), (128, 128)).astype(BF16)
    for ref, side, scale in ((mask_in, 16, 1.0), (mask_out, 8, 0.5)):
        shape = ref.shape
        pixel = lax.broadcasted_iota(jnp.int32, shape, 0) // side
        lane = lax.broadcasted_iota(jnp.int32, shape, 1)
        chosen = jnp.where(lane == (t % 4) * 32 + pixel, 1.0, 0.0).astype(BF16)
        ref[...] = nt(chosen, kept) * scale
    for slot in range(2):
        hid[slot, 0:8] = jnp.zeros((8, MID), F32)
    for ref in ga_fs:
        ref[HALF_WIDE : HALF_WIDE + 8] = jnp.zeros((8, MID), F32)
    acc_b[384:512] = jnp.zeros((128, 128), F32)
    for ref in zskips:
        ref[...] = jnp.zeros(ref.shape, F32)
    w_copies[1].wait()
    wr_h[...] = wr[...] * jnp.asarray(0.5, BF16)

    halo_down = pltpu.make_async_remote_copy(
        odd.at[8], odd.at[0], halo_send.at[0], halo_recv.at[0], device_id=down, device_id_type=MESH
    )
    halo_up = pltpu.make_async_remote_copy(
        ga2.at[0], ga2.at[8], halo_send.at[1], halo_recv.at[1], device_id=up, device_id_type=MESH
    )

    def hidden_pair(k, c):
        i = (k + 7) % 8
        for p in range(2):
            y = 2 * i + p
            x_copy(y).wait()
            for at in range(0, WIDE, 256):
                cols = slice(at, at + 256)
                x = xin[y, at // 16 : (at + 256) // 16].reshape(256, 256)
                h, slope = silu_parts(nn(x, wr_h[...]), mask_in[cols])
                dpre[y, cols] = slope
                hid[p, 8 + at : 8 + at + 256] = h
            target = odd.at[i + 1] if p else even.at[i]
            for v in range(3):
                target[:, v * MID : (v + 1) * MID] = hid[p, pl.ds(7 + v, HALF_WIDE, stride=2)].astype(BF16)

        return c

    lax.fori_loop(0, 8, hidden_pair, 0)
    pl.semaphore_wait(barrier, N_XY - 1 + N_Z - 1 + 3)
    halo_down.start()

    for copy in w_copies[2:]:
        copy.wait()
    for to, of in ((wsp_h, wsp), (we_h, we), (wsc_h, wsc)):
        to[...] = of[...] * jnp.asarray(0.5, BF16)
    for u in range(3):
        tap = u * 3 * MID
        wb[u, 0:MID, 0:MID] = wsp_h[tap + MID : tap + 2 * MID]
        wb[u, 0:MID, MID:] = jnp.zeros((MID, MID), BF16)
        wb[u, MID:, 0:MID] = wsp_h[tap + 2 * MID : tap + 3 * MID]
        wb[u, MID:, MID:] = wsp_h[tap : tap + MID]

    def every_og(i, c):
        og_copy(i).wait()
        return c

    lax.fori_loop(0, 8, every_og, 0)

    def first_stage(n, i):
        half = nn(even[i], wsp_h[384:768]) + nn(odd[i + 1], wsp_h[768:1152]) + nn(odd[i], wsp_h[0:384])
        h, dact = silu_parts(half)
        dacts[n % 3][...] = dact
        gated[i] = h.astype(BF16)
        row = xin[2 * i].reshape(WIDE, 256).astype(F32)
        for side in range(2):
            skip_fs[n % 2][side] = row[:, side * 128 : (side + 1) * 128]
        for side in range(2):
            skip[i, :, side * 128 : (side + 1) * 128] = skip_fs[n % 2][side, pl.ds(0, HALF_WIDE, stride=2)].astype(BF16)

    def second_stage(n, i):
        for row in range(0, HALF_WIDE, 256):
            rows = slice(row, row + 256)
            m = mask_out[rows]
            m = jnp.concatenate([m] * 2, axis=1)
            for col in range(0, 512, 256):
                at = slice(col, col + 256)
                half = nn(gated[i, rows], we_h[:, at]) + nn(skip[i, rows], wsc_h[:, at])
                _, slope = silu_parts(half, m)
                grad = og[i, row // 8 : (row + 256) // 8, :, at].astype(F32).reshape(256, 256)
                gt[i, rows, at] = (grad * slope).astype(BF16)

    def fourth_stage(n, i):
        ga = nt(gt[i], we_h[...]) * dacts[n % 3][...]
        ga2[i, :, 0:MID] = ga.astype(BF16)
        ga_fs[n % 2][0:HALF_WIDE] = ga
        ga2[i, :, MID:] = ga_fs[n % 2][1 : 1 + HALF_WIDE].astype(BF16)

    order = (1, 2, 3, 4, 5, 6, 7, 0)
    for step in range(9):
        if step == 7:
            halo_down.wait_recv()
            odd[0] = odd[0] * jnp.where(t == 0, 0.0, 1.0).astype(BF16)
        if step > 0:
            second_stage(step - 1, order[step - 1])
        if step < 8:
            first_stage(step, order[step])
        if step > 0:
            fourth_stage(step - 1, order[step - 1])
    halo_up.start()

    gt_all = gt[...].reshape(8 * HALF_WIDE, 512)
    part = tn(skip[...].reshape(8 * HALF_WIDE, 256), gt_all)
    for k in range(4):
        acc_a[k * 256 : (k + 1) * 256] = part[:, k * 128 : (k + 1) * 128]
    part = tn(gated[...].reshape(8 * HALF_WIDE, MID), gt_all)
    for k in range(4):
        acc_a[1024 + k * 128 : 1152 + k * 128] = part[:, k * 128 : (k + 1) * 128]
    ga_all = ga2[0:8, :, 0:MID].reshape(8 * HALF_WIDE, MID)
    for u in range(3):
        taps = (odd[0:8], even[...], odd[1:9])[u].reshape(8 * HALF_WIDE, 384)
        part = tn(ga_all, taps)
        for v in range(3):
            tap = u * 3 + v
            to, at = (acc_a, 1536 + tap * 128) if tap < 8 else (acc_b, 0)
            to[at : at + 128] = part[:, v * 128 : (v + 1) * 128]

    def hidden_grad(n, i):
        this = ga2[i]
        for p in range(2):
            if p == 0:
                both = nt(this, wb[1])
            else:
                both = nt(this, wb[2]) + nt(ga2[i + 1], wb[0])
            spreads[n % 2][p, pl.ds(0, HALF_WIDE, stride=2)] = both[:, 0:MID]
            spreads[n % 2][p, pl.ds(1, HALF_WIDE, stride=2)] = both[:, MID:]

    def grad_pair(n, i):
        for p in range(2):
            gp[2 * i + p] = (spreads[n % 2][p] * dpre[2 * i + p]).astype(BF16)

    def grad_pairs(first, last):
        for i in range(first, last + 1):
            if i < last:
                hidden_grad(i, i)
            if i > first:
                grad_pair(i - 1, i - 1)

    def reduce_pairs(first, last):
        rows = (last - first) * 2 * WIDE
        return tn(
            gp[2 * first : 2 * last].reshape(rows, MID), xin[2 * first : 2 * last].reshape(rows, 256)
        )

    def out_pair(i):
        back = nt(gt[i], wsc[...])
        for half in range(2):
            zskips[i % 2][half, pl.ds(0, HALF_WIDE, stride=2)] = back[:, half * 128 : (half + 1) * 128]
        first = nt(gp[2 * i], wr[...]) + jnp.concatenate([zskips[i % 2][0], zskips[i % 2][1]], axis=1)
        out_v[2 * i] = first.astype(BF16).reshape(32, 16, 256)
        second = nt(gp[2 * i + 1], wr[...])
        out_v[2 * i + 1] = second.astype(BF16).reshape(32, 16, 256)

    accs, cores = (acc_a, acc_b), (core_a, core_b)
    xy_outs, xy_ins = (xy_out_a, xy_out_b), (xy_in_a, xy_in_b)
    xy_sends, xy_recvs = (xy_send_a, xy_send_b), (xy_recv_a, xy_recv_b)
    z_ins, dones = (z_in_a, z_in_b), (done_a, done_b)
    z_sends, z_recvs = (z_send_a, z_send_b), (z_recv_a, z_recv_b)
    b_sends, b_recvs = (b_send_a, b_send_b), (b_recv_a, b_recv_b)
    f_sends, f_recvs = (f_send_a, f_send_b), (f_recv_a, f_recv_b)

    def core_copy(part):
        rows = N_XY * CHUNKS[part]
        return pltpu.make_async_remote_copy(
            accs[part].at[pl.ds(pl.multiple_of((1 - core) * rows, 8), rows)], cores[part],
            c_send.at[part], c_recv.at[part], device_id=core_peer, device_id_type=MESH,
        )

    def xy_copy(part, q, slot):
        return pltpu.make_async_remote_copy(
            xy_outs[part].at[q], xy_ins[part].at[slot], xy_sends[part].at[q], xy_recvs[part].at[slot],
            device_id=xy_peer(q), device_id_type=MESH,
        )

    def both_cores(part, q):
        chunk = CHUNKS[part]
        at = pl.multiple_of(q * chunk, 8)
        kept = accs[part][pl.ds(pl.multiple_of(core * (N_XY * chunk) + at, 8), chunk)]
        return kept + cores[part][pl.ds(at, chunk)]

    def send_xy(part):
        for q in xy_to:
            xy_outs[part][q] = both_cores(part, q).astype(BF16)
            xy_copy(part, q, me).start()

    def take_xy(part):
        total = both_cores(part, me)
        for q in xy_from:
            xy_copy(part, q, q).wait_recv()
            total = total + xy_ins[part][q].astype(F32)
        return total

    def z_copy(part, q, slot):
        return pltpu.make_async_remote_copy(
            z_ins[part].at[zi], z_ins[part].at[slot], z_sends[part].at[q], z_recvs[part].at[slot],
            device_id=z_peer(q), device_id_type=MESH,
        )

    def send_z(part):
        z_ins[part][zi] = take_xy(part).astype(BF16)

        for q in z_to:
            z_copy(part, q, zi).start()

    mine = core * N_XY

    def back_copy(part, q, slot):
        return pltpu.make_async_remote_copy(
            dones[part].at[mine + me], dones[part].at[mine + slot], b_sends[part].at[q], b_recvs[part].at[slot],
            device_id=xy_peer(q), device_id_type=MESH,
        )

    def pass_copy(part, q, side):
        return pltpu.make_async_remote_copy(
            dones[part].at[mine + q], dones[part].at[side * N_XY + q], f_sends[part].at[q], f_recvs[part].at[q],
            device_id=core_peer, device_id_type=MESH,
        )

    def send_back(part):
        for q in z_from:
            z_copy(part, q, q).wait_recv()
        whole = z_ins[part][0].astype(F32)
        for q in range(1, N_Z):
            whole = whole + z_ins[part][q].astype(F32)
        dones[part][mine + me] = whole.astype(BF16)

        for q in xy_to:
            back_copy(part, q, me).start()
        pass_copy(part, me, core).start()

    def pass_on(part):
        for q in xy_from:
            back_copy(part, q, q).wait_recv()
            pass_copy(part, q, core).start()

    core_copy(0).start()
    grad_pairs(0, 2)
    core_copy(0).wait_recv()
    send_xy(0)
    halo_up.wait_recv()
    ga2[8] = ga2[8] * jnp.where(t == 31, 0.0, 1.0).astype(BF16)
    grad_pairs(2, 8)
    total = reduce_pairs(0, 8)
    acc_b[128:256] = total[:, 0:128]
    acc_b[256:384] = total[:, 128:256]
    core_copy(1).start()
    for i in range(0, 2):
        out_pair(i)
    core_copy(1).wait_recv()
    send_xy(1)
    send_z(0)
    for i in range(2, 6):
        out_pair(i)
    send_z(1)
    for i in range(6, 8):
        out_pair(i)
    send_back(0)
    send_back(1)
    pass_on(0)
    pass_on(1)

    halo_down.wait_send()
    halo_up.wait_send()
    for part in range(2):
        core_copy(part).wait_send()

    def sent_xy(k, c):
        q = (me + k) % N_XY
        for part in range(2):
            xy_copy(part, q, me).wait_send()
            back_copy(part, q, me).wait_send()
        return c

    lax.fori_loop(1, N_XY, sent_xy, 0)

    def sent_z(k, c):
        for part in range(2):
            z_copy(part, (zi + k) % N_Z, zi).wait_send()
        return c

    lax.fori_loop(1, N_Z, sent_z, 0)

    def passed(k, c):
        q = (me + N_XY - k) % N_XY
        for part in range(2):
            pass_copy(part, q, core).wait_send()
            pass_copy(part, q, 1 - core).wait_recv()
        return c

    lax.fori_loop(0, N_XY, passed, 0)


def write_out(
    out_v, done_a, done_b, ig_hbm, gr_hbm, gsp_hbm, gexp_hbm, gsc_hbm, gr, gsp, gexp, gsc, out_sem, w_sem
):
    copies = [
        pltpu.make_async_copy(out_v.at[y], ig_hbm.at[:, y], out_sem.at[y]) for y in range(ROWS)
    ]
    for copy in copies:
        copy.start()
    part = done_a[...].astype(F32).reshape(2560, 128)
    last = done_b[...].astype(F32).reshape(512, 128)
    for k in range(4):
        gsc[:, k * 128 : (k + 1) * 128] = part[k * 256 : (k + 1) * 256]
        gexp[:, k * 128 : (k + 1) * 128] = part[1024 + k * 128 : 1152 + k * 128]
    for k in range(8):
        gsp[k * 128 : (k + 1) * 128] = part[1536 + k * 128 : 1664 + k * 128].T
    gsp[1024:1152] = last[0:128].T
    for k in range(2):
        gr[k * 128 : (k + 1) * 128] = last[128 + k * 128 : 256 + k * 128].T
    pairs = ((gr, gr_hbm), (gsp, gsp_hbm), (gexp, gexp_hbm), (gsc, gsc_hbm))
    more = [pltpu.make_async_copy(a, b, w_sem.at[k]) for k, (a, b) in enumerate(pairs)]
    for copy in more:
        copy.start()
    for copy in copies + more:
        copy.wait()


def body(slide_tiles, balance_list, output_grad, w_reduce, w_spatial, w_expand, w_shortcut):
    dma = pltpu.SemaphoreType.DMA
    any_spec = pl.BlockSpec(memory_space=pltpu.HBM)
    vmem_spec = pl.BlockSpec(memory_space=pltpu.VMEM)
    out_v, done_a, done_b = pl.pallas_call(
        kernel,
        out_shape=(
            pltpu.VMEM((16, 32, 16, 256), BF16),
            pltpu.VMEM((2 * N_XY, CHUNKS[0], 128), BF16),
            pltpu.VMEM((2 * N_XY, CHUNKS[1], 128), BF16),
        ),
        in_specs=[any_spec] * 7,
        out_specs=(vmem_spec, vmem_spec, vmem_spec),
        scratch_shapes=[
            pltpu.VMEM((16, 32, 16, 256), BF16),
            pltpu.VMEM((8, 32, 8, 512), BF16),
            pltpu.VMEM((256, 128), BF16),
            pltpu.VMEM((1152, 128), BF16),
            pltpu.VMEM((128, 512), BF16),
            pltpu.VMEM((256, 512), BF16),
            pltpu.VMEM((1, 1024), jnp.int32),
            pltpu.VMEM((WIDE, 128), F32),
            pltpu.VMEM((HALF_WIDE, 128), F32),
            pltpu.VMEM((2, WIDE + 16, MID), F32),
            pltpu.VMEM((16, WIDE, MID), F32),
            pltpu.VMEM((8, HALF_WIDE, 384), BF16),
            pltpu.VMEM((9, HALF_WIDE, 384), BF16),
            [pltpu.VMEM((2, WIDE, 128), F32)] * 2,
            pltpu.VMEM((8, HALF_WIDE, 256), BF16),
            pltpu.VMEM((8, HALF_WIDE, MID), BF16),
            pltpu.VMEM((8, HALF_WIDE, 512), BF16),
            pltpu.VMEM((9, HALF_WIDE, 256), BF16),
            [pltpu.VMEM((HALF_WIDE + 8, MID), F32)] * 2,
            pltpu.VMEM((3, 256, 256), BF16),
            [pltpu.VMEM((HALF_WIDE, MID), F32)] * 3,
            [pltpu.VMEM((2, WIDE, MID), F32)] * 2,
            pltpu.VMEM((16, WIDE, MID), BF16),
            [pltpu.VMEM((2, WIDE, 128), F32)] * 2,
            pltpu.VMEM((256, 128), BF16),
            pltpu.VMEM((1152, 128), BF16),
            pltpu.VMEM((128, 512), BF16),
            pltpu.VMEM((256, 512), BF16),
            pltpu.VMEM((2560, 128), F32),
            pltpu.VMEM((512, 128), F32),
            pltpu.VMEM((1280, 128), F32),
            pltpu.VMEM((256, 128), F32),
            pltpu.VMEM((N_XY, 80, 128), BF16),
            pltpu.VMEM((N_XY, 16, 128), BF16),
            pltpu.VMEM((N_XY, 80, 128), BF16),
            pltpu.VMEM((N_XY, 16, 128), BF16),
            pltpu.VMEM((N_Z, 80, 128), BF16),
            pltpu.VMEM((N_Z, 16, 128), BF16),
            dma((16,)),
            dma((8,)),
            dma((5,)),
            dma((2,)),
            dma((2,)),
            dma((2,)),
            dma((2,)),
            *[dma((N_XY,))] * 4,
            *[dma((N_Z,))] * 4,
            *[dma((N_XY,))] * 8,
        ],
        compiler_params=pltpu.CompilerParams(
            collective_id=0, has_side_effects=True, vmem_limit_bytes=59 * 2**20
        ),
    )(slide_tiles[0], balance_list, output_grad[0], w_reduce, w_spatial, w_expand, w_shortcut)
    shapes = ((256, 128), (1152, 128), (128, 512), (256, 512))
    out = pl.pallas_call(
        write_out,
        out_shape=[jax.ShapeDtypeStruct((32, 16, 16, 256), BF16)]
        + [jax.ShapeDtypeStruct(shape, F32) for shape in shapes],
        in_specs=[vmem_spec] * 3,
        out_specs=[any_spec] * 5,
        scratch_shapes=[pltpu.VMEM(shape, F32) for shape in shapes] + [dma((16,)), dma((4,))],
        compiler_params=pltpu.CompilerParams(vmem_limit_bytes=16 * 2**20),
    )(out_v, done_a, done_b)
    return (out[0][None], out[1], out[2], out[3], out[4])


def solution(mesh):
    in_specs = (
        P("slide", "tile", None, None, None),
        P("slide", None),
        P("slide", "tile", None, None, None),
        P(),
        P(),
        P(),
        P(),
    )
    out_specs = (P("slide", "tile", None, None, None), P(), P(), P(), P())
    return jax.shard_map(body, mesh=mesh, in_specs=in_specs, out_specs=out_specs, check_vma=False)
```

```python
import jax
import jax.numpy as jnp
from jax import lax
from jax.experimental import pallas as pl
from jax.experimental.pallas import tpu as pltpu
from jax.sharding import PartitionSpec as P

MESH = pl.DeviceIdType.MESH
F32 = jnp.float32
BF16 = jnp.bfloat16

ROWS = 16
OUT_ROWS = 8
WIDE = 512
HALF_WIDE = 256
MID = 128
N_XY = 16
N_Z = 8
CHUNKS = (80, 16)


def nn(a, b):
    return lax.dot_general(a, b, (((1,), (0,)), ((), ())), preferred_element_type=F32)


def nt(a, b):
    return lax.dot_general(a, b, (((1,), (1,)), ((), ())), preferred_element_type=F32)


def tn(a, b):
    return lax.dot_general(a, b, (((0,), (0,)), ((), ())), preferred_element_type=F32)


def silu_parts(half, scale=None):
    u = jnp.tanh(half)
    twice = 1.0 + u
    if scale is not None:
        twice = twice * scale
    h = half * twice
    return h, twice + h * (1.0 - u)


def kernel(
    x_hbm, bal_hbm, og_hbm, wr_hbm, wsp_hbm, we_hbm, wsc_hbm,
    out_v, done_a, done_b,
    xin, og, wr, wsp, we, wsc, bal,
    mask_in, mask_out, hid, dpre, even, odd, skip_fs, skip, gated, gt, ga2, ga_fs, wb, dacts,
    spreads, gp, zskips, wr_h, wsp_h, we_h, wsc_h,
    acc_a, acc_b, core_a, core_b, xy_out_a, xy_out_b, xy_in_a, xy_in_b, z_in_a, z_in_b,
    x_sem, og_sem, w_sem, halo_send, halo_recv,
    c_send, c_recv, xy_send_a, xy_send_b, xy_recv_a, xy_recv_b,
    z_send_a, z_send_b, z_recv_a, z_recv_b, b_send_a, b_send_b, b_recv_a, b_recv_b,
    f_send_a, f_send_b, f_recv_a, f_recv_b,
):
    s = lax.axis_index("slide")
    t = lax.axis_index("tile")
    y_lo = t // 16
    zi = (t // 2) % N_Z
    core = t % 2
    me = s * 2 + y_lo

    def xy_peer(q):
        return (q // 2, (q % 2) * 16 + t % 16)

    def z_peer(q):
        return (s, y_lo * 16 + q * 2 + core)

    x, y = me // 4, me % 4
    steps = sorted(((a, b) for a in range(4) for b in range(4) if a or b), key=lambda d: -min(d[0], 4 - d[0]) - min(d[1], 4 - d[1]))
    xy_to = [(x + a) % 4 * 4 + (y + b) % 4 for a, b in steps]
    xy_from = [(x + 4 - a) % 4 * 4 + (y + 4 - b) % 4 for a, b in steps]
    z_to = [(zi + k) % N_Z for k in (4, 3, 5, 2, 6, 1, 7)]
    z_from = [(zi + N_Z - k) % N_Z for k in (4, 3, 5, 2, 6, 1, 7)]

    core_peer = (s, t + 1 - 2 * core)
    down = (s, (t + 1) % 32)
    up = (s, (t + 31) % 32)

    def x_copy(y):
        return pltpu.make_async_copy(x_hbm.at[:, y], xin.at[y], x_sem.at[y])

    def og_copy(i):
        return pltpu.make_async_copy(og_hbm.at[:, i], og.at[i], og_sem.at[i])

    w_copies = [
        pltpu.make_async_copy(a, b, w_sem.at[k])
        for k, (a, b) in enumerate(
            [(bal_hbm, bal), (wr_hbm, wr), (wsp_hbm, wsp), (we_hbm, we), (wsc_hbm, wsc)]
        )
    ]
    w_copies[0].start()
    w_copies[1].start()
    x_copy(14).start()
    x_copy(15).start()

    def start_x(y, c):
        x_copy(y).start()
        return c

    lax.fori_loop(0, ROWS - 2, start_x, 0)
    for copy in w_copies[2:]:
        copy.start()

    def start_og(i, c):
        og_copy(i).start()
        return c

    lax.fori_loop(0, OUT_ROWS, start_og, 0)

    barrier = pltpu.get_barrier_semaphore()

    def greet_xy(k, c):
        pl.semaphore_signal(barrier, 1, device_id=xy_peer((me + k) % N_XY), device_id_type=MESH)
        return c

    def greet_z(k, c):
        pl.semaphore_signal(barrier, 1, device_id=z_peer((zi + k) % N_Z), device_id_type=MESH)
        return c

    lax.fori_loop(1, N_XY, greet_xy, 0)
    lax.fori_loop(1, N_Z, greet_z, 0)
    for peer in (core_peer, down, up):
        pl.semaphore_signal(barrier, 1, device_id=peer, device_id_type=MESH)

    w_copies[0].wait()
    window = bal[:, pl.ds(pl.multiple_of((t // 4) * 128, 128), 128)]
    kept = jnp.broadcast_to(jnp.where(window >= 0, 1.0, 0.0).astype(F32), (128, 128)).astype(BF16)
    for ref, side, scale in ((mask_in, 16, 1.0), (mask_out, 8, 0.5)):
        shape = ref.shape
        pixel = lax.broadcasted_iota(jnp.int32, shape, 0) // side
        lane = lax.broadcasted_iota(jnp.int32, shape, 1)
        chosen = jnp.where(lane == (t % 4) * 32 + pixel, 1.0, 0.0).astype(BF16)
        ref[...] = nt(chosen, kept) * scale
    for slot in range(2):
        hid[slot, 0:8] = jnp.zeros((8, MID), F32)
    for ref in ga_fs:
        ref[HALF_WIDE : HALF_WIDE + 8] = jnp.zeros((8, MID), F32)
    acc_b[384:512] = jnp.zeros((128, 128), F32)
    for ref in zskips:
        ref[...] = jnp.zeros(ref.shape, F32)
    w_copies[1].wait()
    wr_h[...] = wr[...] * jnp.asarray(0.5, BF16)

    halo_down = pltpu.make_async_remote_copy(
        odd.at[8], odd.at[0], halo_send.at[0], halo_recv.at[0], device_id=down, device_id_type=MESH
    )
    halo_up = pltpu.make_async_remote_copy(
        ga2.at[0], ga2.at[8], halo_send.at[1], halo_recv.at[1], device_id=up, device_id_type=MESH
    )

    def hidden_pair(k, c):
        i = (k + 7) % 8
        for p in range(2):
            y = 2 * i + p
            x_copy(y).wait()
            for at in range(0, WIDE, 256):
                cols = slice(at, at + 256)
                x = xin[y, at // 16 : (at + 256) // 16].reshape(256, 256)
                h, slope = silu_parts(nn(x, wr_h[...]), mask_in[cols])
                dpre[y, cols] = slope
                hid[p, 8 + at : 8 + at + 256] = h
            target = odd.at[i + 1] if p else even.at[i]
            for v in range(3):
                target[:, v * MID : (v + 1) * MID] = hid[p, pl.ds(7 + v, HALF_WIDE, stride=2)].astype(BF16)

        return c

    lax.fori_loop(0, 8, hidden_pair, 0)
    pl.semaphore_wait(barrier, N_XY - 1 + N_Z - 1 + 3)
    halo_down.start()

    for copy in w_copies[2:]:
        copy.wait()
    for to, of in ((wsp_h, wsp), (we_h, we), (wsc_h, wsc)):
        to[...] = of[...] * jnp.asarray(0.5, BF16)
    for u in range(3):
        tap = u * 3 * MID
        wb[u, 0:MID, 0:MID] = wsp_h[tap + MID : tap + 2 * MID]
        wb[u, 0:MID, MID:] = jnp.zeros((MID, MID), BF16)
        wb[u, MID:, 0:MID] = wsp_h[tap + 2 * MID : tap + 3 * MID]
        wb[u, MID:, MID:] = wsp_h[tap : tap + MID]

    def every_og(i, c):
        og_copy(i).wait()
        return c

    lax.fori_loop(0, 8, every_og, 0)

    def first_stage(n, i):
        half = nn(even[i], wsp_h[384:768]) + nn(odd[i + 1], wsp_h[768:1152]) + nn(odd[i], wsp_h[0:384])
        h, dact = silu_parts(half)
        dacts[n % 3][...] = dact
        gated[i] = h.astype(BF16)
        row = xin[2 * i].reshape(WIDE, 256).astype(F32)
        for side in range(2):
            skip_fs[n % 2][side] = row[:, side * 128 : (side + 1) * 128]
        for side in range(2):
            skip[i, :, side * 128 : (side + 1) * 128] = skip_fs[n % 2][side, pl.ds(0, HALF_WIDE, stride=2)].astype(BF16)

    def second_stage(n, i):
        for row in range(0, HALF_WIDE, 256):
            rows = slice(row, row + 256)
            m = mask_out[rows]
            m = jnp.concatenate([m] * 2, axis=1)
            for col in range(0, 512, 256):
                at = slice(col, col + 256)
                half = nn(gated[i, rows], we_h[:, at]) + nn(skip[i, rows], wsc_h[:, at])
                _, slope = silu_parts(half, m)
                grad = og[i, row // 8 : (row + 256) // 8, :, at].astype(F32).reshape(256, 256)
                gt[i, rows, at] = (grad * slope).astype(BF16)

    def fourth_stage(n, i):
        ga = nt(gt[i], we_h[...]) * dacts[n % 3][...]
        ga2[i, :, 0:MID] = ga.astype(BF16)
        ga_fs[n % 2][0:HALF_WIDE] = ga
        ga2[i, :, MID:] = ga_fs[n % 2][1 : 1 + HALF_WIDE].astype(BF16)

    order = (1, 2, 3, 4, 5, 6, 7, 0)
    for step in range(9):
        if step == 7:
            halo_down.wait_recv()
            odd[0] = odd[0] * jnp.where(t == 0, 0.0, 1.0).astype(BF16)
        if step > 0:
            second_stage(step - 1, order[step - 1])
        if step < 8:
            first_stage(step, order[step])
        if step > 0:
            fourth_stage(step - 1, order[step - 1])
    halo_up.start()

    gt_all = gt[...].reshape(8 * HALF_WIDE, 512)
    part = tn(skip[...].reshape(8 * HALF_WIDE, 256), gt_all)
    for k in range(4):
        acc_a[k * 256 : (k + 1) * 256] = part[:, k * 128 : (k + 1) * 128]
    part = tn(gated[...].reshape(8 * HALF_WIDE, MID), gt_all)
    for k in range(4):
        acc_a[1024 + k * 128 : 1152 + k * 128] = part[:, k * 128 : (k + 1) * 128]
    ga_all = ga2[0:8, :, 0:MID].reshape(8 * HALF_WIDE, MID)
    for u in range(3):
        taps = (odd[0:8], even[...], odd[1:9])[u].reshape(8 * HALF_WIDE, 384)
        part = tn(ga_all, taps)
        for v in range(3):
            tap = u * 3 + v
            to, at = (acc_a, 1536 + tap * 128) if tap < 8 else (acc_b, 0)
            to[at : at + 128] = part[:, v * 128 : (v + 1) * 128]

    def hidden_grad(n, i):
        this = ga2[i]
        for p in range(2):
            if p == 0:
                both = nt(this, wb[1])
            else:
                both = nt(this, wb[2]) + nt(ga2[i + 1], wb[0])
            spreads[n % 2][p, pl.ds(0, HALF_WIDE, stride=2)] = both[:, 0:MID]
            spreads[n % 2][p, pl.ds(1, HALF_WIDE, stride=2)] = both[:, MID:]

    def grad_pair(n, i):
        for p in range(2):
            gp[2 * i + p] = (spreads[n % 2][p] * dpre[2 * i + p]).astype(BF16)

    def grad_pairs(first, last):
        for i in range(first, last + 1):
            if i < last:
                hidden_grad(i, i)
            if i > first:
                grad_pair(i - 1, i - 1)

    def reduce_pairs(first, last):
        rows = (last - first) * 2 * WIDE
        return tn(
            gp[2 * first : 2 * last].reshape(rows, MID), xin[2 * first : 2 * last].reshape(rows, 256)
        )

    def out_pair(i):
        back = nt(gt[i], wsc[...])
        for half in range(2):
            zskips[i % 2][half, pl.ds(0, HALF_WIDE, stride=2)] = back[:, half * 128 : (half + 1) * 128]
        first = nt(gp[2 * i], wr[...]) + jnp.concatenate([zskips[i % 2][0], zskips[i % 2][1]], axis=1)
        out_v[:, 2 * i] = first.astype(BF16).reshape(32, 16, 256)
        second = nt(gp[2 * i + 1], wr[...])
        out_v[:, 2 * i + 1] = second.astype(BF16).reshape(32, 16, 256)

    accs, cores = (acc_a, acc_b), (core_a, core_b)
    xy_outs, xy_ins = (xy_out_a, xy_out_b), (xy_in_a, xy_in_b)
    xy_sends, xy_recvs = (xy_send_a, xy_send_b), (xy_recv_a, xy_recv_b)
    z_ins, dones = (z_in_a, z_in_b), (done_a, done_b)
    z_sends, z_recvs = (z_send_a, z_send_b), (z_recv_a, z_recv_b)
    b_sends, b_recvs = (b_send_a, b_send_b), (b_recv_a, b_recv_b)
    f_sends, f_recvs = (f_send_a, f_send_b), (f_recv_a, f_recv_b)

    def core_copy(part):
        rows = N_XY * CHUNKS[part]
        return pltpu.make_async_remote_copy(
            accs[part].at[pl.ds(pl.multiple_of((1 - core) * rows, 8), rows)], cores[part],
            c_send.at[part], c_recv.at[part], device_id=core_peer, device_id_type=MESH,
        )

    def xy_copy(part, q, slot):
        return pltpu.make_async_remote_copy(
            xy_outs[part].at[q], xy_ins[part].at[slot], xy_sends[part].at[q], xy_recvs[part].at[slot],
            device_id=xy_peer(q), device_id_type=MESH,
        )

    def both_cores(part, q):
        chunk = CHUNKS[part]
        at = pl.multiple_of(q * chunk, 8)
        kept = accs[part][pl.ds(pl.multiple_of(core * (N_XY * chunk) + at, 8), chunk)]
        return kept + cores[part][pl.ds(at, chunk)]

    def send_xy(part):
        for q in xy_to:
            xy_outs[part][q] = both_cores(part, q).astype(BF16)
            xy_copy(part, q, me).start()

    def take_xy(part):
        total = both_cores(part, me)
        for q in xy_from:
            xy_copy(part, q, q).wait_recv()
            total = total + xy_ins[part][q].astype(F32)
        return total

    def z_copy(part, q, slot):
        return pltpu.make_async_remote_copy(
            z_ins[part].at[zi], z_ins[part].at[slot], z_sends[part].at[q], z_recvs[part].at[slot],
            device_id=z_peer(q), device_id_type=MESH,
        )

    def send_z(part):
        z_ins[part][zi] = take_xy(part).astype(BF16)

        for q in z_to:
            z_copy(part, q, zi).start()

    mine = core * N_XY

    def back_copy(part, q, slot):
        return pltpu.make_async_remote_copy(
            dones[part].at[mine + me], dones[part].at[mine + slot], b_sends[part].at[q], b_recvs[part].at[slot],
            device_id=xy_peer(q), device_id_type=MESH,
        )

    def pass_copy(part, q, side):
        return pltpu.make_async_remote_copy(
            dones[part].at[mine + q], dones[part].at[side * N_XY + q], f_sends[part].at[q], f_recvs[part].at[q],
            device_id=core_peer, device_id_type=MESH,
        )

    def send_back(part):
        for q in z_from:
            z_copy(part, q, q).wait_recv()
        whole = z_ins[part][0].astype(F32)
        for q in range(1, N_Z):
            whole = whole + z_ins[part][q].astype(F32)
        dones[part][mine + me] = whole.astype(BF16)

        for q in xy_to:
            back_copy(part, q, me).start()
        pass_copy(part, me, core).start()

    def pass_on(part):
        for q in xy_from:
            back_copy(part, q, q).wait_recv()
            pass_copy(part, q, core).start()

    core_copy(0).start()
    grad_pairs(0, 2)
    core_copy(0).wait_recv()
    send_xy(0)
    halo_up.wait_recv()
    ga2[8] = ga2[8] * jnp.where(t == 31, 0.0, 1.0).astype(BF16)
    grad_pairs(2, 8)
    total = reduce_pairs(0, 8)
    acc_b[128:256] = total[:, 0:128]
    acc_b[256:384] = total[:, 128:256]
    core_copy(1).start()
    for i in range(0, 2):
        out_pair(i)
    core_copy(1).wait_recv()
    send_xy(1)
    send_z(0)
    for i in range(2, 6):
        out_pair(i)
    send_z(1)
    for i in range(6, 8):
        out_pair(i)
    send_back(0)
    send_back(1)
    pass_on(0)
    pass_on(1)

    halo_down.wait_send()
    halo_up.wait_send()
    for part in range(2):
        core_copy(part).wait_send()

    def sent_xy(k, c):
        q = (me + k) % N_XY
        for part in range(2):
            xy_copy(part, q, me).wait_send()
            back_copy(part, q, me).wait_send()
        return c

    lax.fori_loop(1, N_XY, sent_xy, 0)

    def sent_z(k, c):
        for part in range(2):
            z_copy(part, (zi + k) % N_Z, zi).wait_send()
        return c

    lax.fori_loop(1, N_Z, sent_z, 0)

    def passed(k, c):
        q = (me + N_XY - k) % N_XY
        for part in range(2):
            pass_copy(part, q, core).wait_send()
            pass_copy(part, q, 1 - core).wait_recv()
        return c

    lax.fori_loop(0, N_XY, passed, 0)


def write_out(
    out_v, done_a, done_b, ig_hbm, gr_hbm, gsp_hbm, gexp_hbm, gsc_hbm, gr, gsp, gexp, gsc, out_sem, w_sem
):
    copies = [
        pltpu.make_async_copy(out_v.at[8 * k : 8 * k + 8], ig_hbm.at[8 * k : 8 * k + 8], out_sem.at[k]) for k in range(4)
    ]
    for copy in copies:
        copy.start()
    part = done_a[...].astype(F32).reshape(2560, 128)
    last = done_b[...].astype(F32).reshape(512, 128)
    for k in range(4):
        gsc[:, k * 128 : (k + 1) * 128] = part[k * 256 : (k + 1) * 256]
        gexp[:, k * 128 : (k + 1) * 128] = part[1024 + k * 128 : 1152 + k * 128]
    for k in range(8):
        gsp[k * 128 : (k + 1) * 128] = part[1536 + k * 128 : 1664 + k * 128].T
    gsp[1024:1152] = last[0:128].T
    for k in range(2):
        gr[k * 128 : (k + 1) * 128] = last[128 + k * 128 : 256 + k * 128].T
    pairs = ((gr, gr_hbm), (gsp, gsp_hbm), (gexp, gexp_hbm), (gsc, gsc_hbm))
    more = [pltpu.make_async_copy(a, b, w_sem.at[k]) for k, (a, b) in enumerate(pairs)]
    for copy in more:
        copy.start()
    for copy in copies + more:
        copy.wait()


def body(slide_tiles, balance_list, output_grad, w_reduce, w_spatial, w_expand, w_shortcut):
    dma = pltpu.SemaphoreType.DMA
    any_spec = pl.BlockSpec(memory_space=pltpu.HBM)
    vmem_spec = pl.BlockSpec(memory_space=pltpu.VMEM)
    out_v, done_a, done_b = pl.pallas_call(
        kernel,
        out_shape=(
            pltpu.VMEM((32, 16, 16, 256), BF16),
            pltpu.VMEM((2 * N_XY, CHUNKS[0], 128), BF16),
            pltpu.VMEM((2 * N_XY, CHUNKS[1], 128), BF16),
        ),
        in_specs=[any_spec] * 7,
        out_specs=(vmem_spec, vmem_spec, vmem_spec),
        scratch_shapes=[
            pltpu.VMEM((16, 32, 16, 256), BF16),
            pltpu.VMEM((8, 32, 8, 512), BF16),
            pltpu.VMEM((256, 128), BF16),
            pltpu.VMEM((1152, 128), BF16),
            pltpu.VMEM((128, 512), BF16),
            pltpu.VMEM((256, 512), BF16),
            pltpu.VMEM((1, 1024), jnp.int32),
            pltpu.VMEM((WIDE, 128), F32),
            pltpu.VMEM((HALF_WIDE, 128), F32),
            pltpu.VMEM((2, WIDE + 16, MID), F32),
            pltpu.VMEM((16, WIDE, MID), F32),
            pltpu.VMEM((8, HALF_WIDE, 384), BF16),
            pltpu.VMEM((9, HALF_WIDE, 384), BF16),
            [pltpu.VMEM((2, WIDE, 128), F32)] * 2,
            pltpu.VMEM((8, HALF_WIDE, 256), BF16),
            pltpu.VMEM((8, HALF_WIDE, MID), BF16),
            pltpu.VMEM((8, HALF_WIDE, 512), BF16),
            pltpu.VMEM((9, HALF_WIDE, 256), BF16),
            [pltpu.VMEM((HALF_WIDE + 8, MID), F32)] * 2,
            pltpu.VMEM((3, 256, 256), BF16),
            [pltpu.VMEM((HALF_WIDE, MID), F32)] * 3,
            [pltpu.VMEM((2, WIDE, MID), F32)] * 2,
            pltpu.VMEM((16, WIDE, MID), BF16),
            [pltpu.VMEM((2, WIDE, 128), F32)] * 2,
            pltpu.VMEM((256, 128), BF16),
            pltpu.VMEM((1152, 128), BF16),
            pltpu.VMEM((128, 512), BF16),
            pltpu.VMEM((256, 512), BF16),
            pltpu.VMEM((2560, 128), F32),
            pltpu.VMEM((512, 128), F32),
            pltpu.VMEM((1280, 128), F32),
            pltpu.VMEM((256, 128), F32),
            pltpu.VMEM((N_XY, 80, 128), BF16),
            pltpu.VMEM((N_XY, 16, 128), BF16),
            pltpu.VMEM((N_XY, 80, 128), BF16),
            pltpu.VMEM((N_XY, 16, 128), BF16),
            pltpu.VMEM((N_Z, 80, 128), BF16),
            pltpu.VMEM((N_Z, 16, 128), BF16),
            dma((16,)),
            dma((8,)),
            dma((5,)),
            dma((2,)),
            dma((2,)),
            dma((2,)),
            dma((2,)),
            *[dma((N_XY,))] * 4,
            *[dma((N_Z,))] * 4,
            *[dma((N_XY,))] * 8,
        ],
        compiler_params=pltpu.CompilerParams(
            collective_id=0, has_side_effects=True, vmem_limit_bytes=59 * 2**20
        ),
    )(slide_tiles[0], balance_list, output_grad[0], w_reduce, w_spatial, w_expand, w_shortcut)
    shapes = ((256, 128), (1152, 128), (128, 512), (256, 512))
    out = pl.pallas_call(
        write_out,
        out_shape=[jax.ShapeDtypeStruct((32, 16, 16, 256), BF16)]
        + [jax.ShapeDtypeStruct(shape, F32) for shape in shapes],
        in_specs=[vmem_spec] * 3,
        out_specs=[any_spec] * 5,
        scratch_shapes=[pltpu.VMEM(shape, F32) for shape in shapes] + [dma((4,)), dma((4,))],
        compiler_params=pltpu.CompilerParams(vmem_limit_bytes=16 * 2**20),
    )(out_v, done_a, done_b)
    return (out[0][None], out[1], out[2], out[3], out[4])


def solution(mesh):
    in_specs = (
        P("slide", "tile", None, None, None),
        P("slide", None),
        P("slide", "tile", None, None, None),
        P(),
        P(),
        P(),
        P(),
    )
    out_specs = (P("slide", "tile", None, None, None), P(), P(), P(), P())
    return jax.shard_map(body, mesh=mesh, in_specs=in_specs, out_specs=out_specs, check_vma=False)
```
